256 devices in a mesh: pool: 32 (over y, x, core), head: 8 (over z).
Axes of the slice: x: 4, y: 4, z: 8, core: 2. Of those that a mesh axis runs over, the one named last changes fastest.
Arguments:
- queries: bfloat16 [32, 8, 2048], P('pool', 'head')
- keys: bfloat16 [2048, 8, 256, 128], P('pool', 'head'), may hold values from -6 to 6
- values: bfloat16 [2048, 8, 256, 128], P('pool', 'head'), may hold values from -6 to 6
- page_table: int32 [32, 64], replicated, may hold values from -1 to 2047, as said below
- lengths: int32 [32], replicated, may hold values from 1 to 16384, as said below
Outputs:
- attended: bfloat16 [32, 8, 2048], P('pool', 'head')
The draws below stay inside these ranges and needn't reach their ends.
Inputs may be any that keep to these rules, and one draw needn't show every extreme that they name: `page_table`: each request names its pages in entries 0 .. ceil(lengths / 256) - 1 and -1 after them; no pool page is named twice; some request has exactly 64 pages. `lengths`: some request has exactly 16384 tokens.
All inputs are finite; a program needn't handle non-finite values.
Results may differ from the reference program's by a relative error of at most 0.015.
Values may be sent and summed in bfloat16 or wider, within the bound.
No kernel may reach another device: no remote copies, remote signals or barrier semaphores. Data moves between devices by JAX's collectives and lax.ppermute only.
A program may use at most 64 MiB of HBM per device.

```python
import jax
import jax.numpy as jnp
from jax import lax

KVH = 8
GROUP = 16
HD = 128
PAGE = 256
MAXP = 64
PAGES_DEV = 64
REQS = 32
TOTAL_PAGES = 2048


def layout(key):
    keys_all = jax.random.split(key, 4)
    counts = jax.random.randint(keys_all[0], (REQS,), 1, MAXP + 1)
    largest = jax.random.randint(keys_all[1], (), 0, REQS)
    counts = counts.at[largest].set(MAXP)
    ends = jnp.cumsum(counts)
    starts = ends - counts
    slots = jnp.arange(TOTAL_PAGES, dtype=jnp.int32)
    factor = 1 + slots // PAGES_DEV % 4
    priority = jax.random.randint(keys_all[2], (TOTAL_PAGES,), 0, 1024) * factor * TOTAL_PAGES + slots
    order = jnp.argsort(priority, stable=True).astype(jnp.int32)
    position = jnp.arange(MAXP, dtype=jnp.int32)
    wanted = jnp.clip(starts[:, None] + position[None, :], 0, TOTAL_PAGES - 1)
    table = jnp.where(position[None, :] < counts[:, None], order[wanted], -1)
    tail = jax.random.randint(keys_all[3], (REQS,), 1, PAGE + 1)
    tail = tail.at[largest].set(PAGE)
    lengths = (counts - 1) * PAGE + tail
    return (table.astype(jnp.int32), lengths.astype(jnp.int32))


def draw_page_table(key, part):
    return layout(key)[0]


def draw_lengths(key, part):
    return layout(key)[1]


def draw_queries(key, part):
    key = jax.random.fold_in(key, 7)
    base = jax.random.normal(key, (REQS, KVH, GROUP * HD), jnp.float32)
    return base.astype(jnp.bfloat16)


def levels(key, shape, pieces, smallest, top_value):
    gain = 1.0
    for dim, parts in pieces:
        draws = jax.random.uniform(jax.random.fold_in(jax.random.fold_in(key, 6), dim), (parts,), jnp.float32, smallest / len(pieces), top_value / len(pieces))
        gain = gain * jnp.repeat(jnp.exp(draws), shape[dim] // parts).reshape((-1,) + (1,) * (len(shape) - 1 - dim))
    return gain


def bell_draw(own_key, dims, spread, bound, cuts=(), kind=jnp.bfloat16):
    values = spread * jax.random.normal(own_key, dims, jnp.float32)
    if cuts:
        values = values * levels(own_key, dims, cuts, -0.22, 0.18)
    return jnp.clip(values, -bound, bound).astype(kind)


def setup_inputs(seed: int = 0) -> dict:
    key_of = jax.random.split(jax.random.key(seed), 6)
    queries = draw_queries(jax.random.fold_in(key_of[5], 71), 0)
    keys = bell_draw(key_of[1], (TOTAL_PAGES, KVH, PAGE, HD), 1.0, 6.0, ((0, 32), (1, 8)))
    values = bell_draw(key_of[2], (TOTAL_PAGES, KVH, PAGE, HD), 1.0, 6.0, ((0, 32), (1, 8)))
    page_table = draw_page_table(jax.random.fold_in(key_of[5], 71), 0)
    lengths = draw_lengths(jax.random.fold_in(key_of[5], 71), 0)
    return dict(queries=queries, keys=keys, values=values, page_table=page_table, lengths=lengths)


def reference(queries, keys, values, page_table, lengths):
    scale = HD ** -0.5

    def one_request(index):
        pages = jnp.maximum(page_table[index], 0).astype(jnp.int32)
        key_rows = keys[pages].transpose(1, 0, 2, 3).reshape(KVH, MAXP * PAGE, HD)
        value_rows = values[pages].transpose(1, 0, 2, 3).reshape(KVH, MAXP * PAGE, HD)
        query = queries[index].reshape(KVH, GROUP, HD)
        scores = jnp.einsum("kgd,ktd->kgt", query.astype(jnp.float32), key_rows.astype(jnp.float32)) * scale
        live = jnp.arange(MAXP * PAGE, dtype=jnp.int32) < lengths[index]
        scores = jnp.where(live[None, None, :], scores, -1e30)
        top = jnp.max(scores, axis=-1)
        weights = jnp.where(live[None, None, :], jnp.exp(scores - top[..., None]), 0.0)
        total = jnp.sum(weights, axis=-1)
        rounded = lax.optimization_barrier(weights.astype(jnp.bfloat16))
        numer = jnp.einsum("kgt,ktd->kgd", rounded.astype(jnp.float32), value_rows.astype(jnp.float32))
        return (numer / total[..., None]).reshape(KVH, GROUP * HD).astype(jnp.bfloat16)

    return lax.map(one_request, jnp.arange(REQS, dtype=jnp.int32))
```

```python
import jax
import jax.numpy as jnp
from jax import lax
from jax.experimental import pallas as pl
from jax.experimental.pallas import tpu as pltpu
from jax.sharding import PartitionSpec as P

MASKED = -3.0e38
EMPTY = -1.5e38
STAT_ROWS = 8


def three_parts(x):
    high = x.astype(jnp.bfloat16).astype(jnp.float32)
    rest = x - high
    middle = rest.astype(jnp.bfloat16).astype(jnp.float32)
    return high, middle, rest - middle


def attend_kernel(owner_ref, live_ref, q_ref, k_ref, v_ref, out_ref, s_ref, mx_ref, sum_ref, acc_ref):
    pages, page_len, head_dim = k_ref.shape
    requests, group, _ = q_ref.shape
    factor = head_dim ** (-0.5) * 1.4426950408889634
    token = lax.broadcasted_iota(jnp.int32, (group, page_len), 1)
    halves = page_len // head_dim
    mx_ref[...] = jnp.full(mx_ref.shape, EMPTY, jnp.float32)
    sum_ref[...] = jnp.zeros(sum_ref.shape, jnp.float32)
    acc_ref[...] = jnp.zeros(acc_ref.shape, jnp.float32)

    def score(p, carry):
        owner = owner_ref[p]
        s = lax.dot_general(
            q_ref[owner], k_ref[p], (((1,), (1,)), ((), ())), preferred_element_type=jnp.float32
        )
        s = jnp.where(token < live_ref[p], s, MASKED)
        s_ref[p] = s
        top = s[:, :head_dim]
        for h in range(1, halves):
            top = jnp.maximum(top, s[:, h * head_dim : (h + 1) * head_dim])
        mx_ref[owner] = jnp.maximum(mx_ref[owner], top)
        return carry

    lax.fori_loop(0, pages, score, 0, unroll=8)
    mx_ref[...] = jnp.broadcast_to(jnp.max(mx_ref[...], axis=-1, keepdims=True), mx_ref.shape)

    def weigh(p, carry):
        owner = owner_ref[p]
        top = mx_ref[owner]
        parts = [
            jnp.exp2((s_ref[p, :, h * head_dim : (h + 1) * head_dim] - top) * factor)
            for h in range(halves)
        ]
        sum_ref[owner] += sum(parts)
        weights = jnp.concatenate(parts, axis=1).astype(jnp.bfloat16)
        acc_ref[owner] += jnp.dot(weights, v_ref[p], preferred_element_type=jnp.float32)
        return carry

    lax.fori_loop(0, pages, weigh, 0, unroll=8)
    out_ref[:, :group, :] = acc_ref[...].astype(jnp.bfloat16)
    total = jnp.broadcast_to(jnp.sum(sum_ref[...], axis=-1, keepdims=True), sum_ref.shape)
    lane = lax.broadcasted_iota(jnp.int32, sum_ref.shape, 2)
    row = lax.broadcasted_iota(jnp.int32, sum_ref.shape, 1)
    stats = jnp.zeros(sum_ref.shape, jnp.float32)
    for k, part in enumerate(three_parts(mx_ref[...]) + three_parts(total)):
        stats = jnp.where(lane == row + k * group, part, stats)
    stats = jnp.sum(stats, axis=1, keepdims=True)
    out_ref[:, group:, :] = jnp.broadcast_to(stats, (requests, STAT_ROWS, head_dim)).astype(jnp.bfloat16)


def join_kernel(parts_ref, out_ref, *, group, factor):
    sources, _, head_dim = parts_ref.shape
    stats = parts_ref[:, group:, :].astype(jnp.float32)[:, 0, :]
    peak = stats[:, :group] + stats[:, group : 2 * group] + stats[:, 2 * group : 3 * group]
    total = (
        stats[:, 3 * group : 4 * group] + stats[:, 4 * group : 5 * group] + stats[:, 5 * group : 6 * group]
    )
    weight = jnp.exp2((peak - jnp.max(peak, axis=0, keepdims=True)) * factor)
    weight = weight / jnp.sum(weight * total, axis=0, keepdims=True)
    weight = weight.T
    result = jnp.zeros((group, head_dim), jnp.float32)
    for s in range(sources):
        result += weight[:, s : s + 1] * parts_ref[s, :group, :].astype(jnp.float32)
    for g in range(group):
        out_ref[0, :, g * head_dim : (g + 1) * head_dim] = result[g : g + 1, :].astype(jnp.bfloat16)


def per_device(queries, keys, values, page_table, lengths):
    pages, _, page_len, head_dim = keys.shape
    group = queries.shape[2] // head_dim
    requests, most_pages = page_table.shape
    factor = head_dim ** (-0.5) * 1.4426950408889634
    spread = jnp.broadcast_to(queries.reshape(1, group, head_dim), (requests, group, head_dim))
    query_all = lax.all_to_all(spread, "pool", 0, 0, tiled=True)
    slot_ids = lax.axis_index("pool") * pages + jnp.arange(pages, dtype=jnp.int32)
    match = page_table[:, :, None] == slot_ids[None, None, :]
    request_ids = jnp.arange(requests, dtype=jnp.int32)
    left = lengths[:, None] - page_len * jnp.arange(most_pages, dtype=jnp.int32)[None, :]
    owner = jnp.sum(jnp.where(match, request_ids[:, None, None], 0), axis=(0, 1))
    live = jnp.sum(jnp.where(match, left[:, :, None], 0), axis=(0, 1))
    vmem = pl.BlockSpec(memory_space=pltpu.VMEM)
    smem = pl.BlockSpec(memory_space=pltpu.SMEM)
    partial = pl.pallas_call(
        attend_kernel,
        out_shape=jax.ShapeDtypeStruct((requests, group + STAT_ROWS, head_dim), jnp.bfloat16),
        in_specs=[smem, smem, vmem, vmem, vmem],
        out_specs=vmem,
        scratch_shapes=[
            pltpu.VMEM((pages, group, page_len), jnp.float32),
            pltpu.VMEM((requests, group, head_dim), jnp.float32),
            pltpu.VMEM((requests, group, head_dim), jnp.float32),
            pltpu.VMEM((requests, group, head_dim), jnp.float32),
        ],
        compiler_params=pltpu.CompilerParams(vmem_limit_bytes=24 * 1024 * 1024),
    )(owner, live, query_all, keys.reshape(pages, page_len, head_dim), values.reshape(pages, page_len, head_dim))
    received = lax.all_to_all(partial, "pool", 0, 0, tiled=True)

    def join(parts_ref, out_ref):
        join_kernel(parts_ref, out_ref, group=group, factor=factor)

    return pl.pallas_call(
        join,
        out_shape=jax.ShapeDtypeStruct((1, 1, group * head_dim), jnp.bfloat16),
        in_specs=[vmem],
        out_specs=vmem,
    )(received)


def solution(mesh):
    placed = (
        P("pool", "head", None),
        P("pool", "head", None, None),
        P("pool", "head", None, None),
        P(),
        P(),
    )
    return jax.shard_map(
        per_device, mesh=mesh, in_specs=placed, out_specs=P("pool", "head", None), check_vma=False
    )
```

```python
import jax
import jax.numpy as jnp
from jax import lax
from jax.experimental import pallas as pl
from jax.experimental.pallas import tpu as pltpu
from jax.sharding import PartitionSpec as P

MASKED = -3.0e38
EMPTY = -1.5e38
STAT_ROWS = 8
CODE = 512
EARLY = 48
CHUNKS = 2
MIB = 1024 * 1024
LOG2E = 1.4426950408889634


def three_parts(x):
    high = x.astype(jnp.bfloat16).astype(jnp.float32)
    rest = x - high
    middle = rest.astype(jnp.bfloat16).astype(jnp.float32)
    return high, middle, rest - middle


def spread_kernel(q_hbm, out_ref, q_ref, sem):
    _, group, head_dim = out_ref.shape
    copy = pltpu.make_async_copy(q_hbm, q_ref, sem)
    copy.start()
    copy.wait()
    rows = [q_ref[0, :, g * head_dim : (g + 1) * head_dim].astype(jnp.float32) for g in range(group)]
    tile = jnp.concatenate(rows, axis=0).astype(jnp.bfloat16)
    out_ref[...] = jnp.broadcast_to(tile[None], out_ref.shape)


def prepare_kernel(length_hbm, table_hbm, k_hbm, code_ref, early_ref, length_ref, table_ref, sems):
    pages, page_len, _ = k_hbm.shape
    requests, most_pages = table_ref.shape
    lengths = pltpu.make_async_copy(length_hbm, length_ref, sems.at[0])
    table = pltpu.make_async_copy(table_hbm, table_ref, sems.at[1])
    early = pltpu.make_async_copy(k_hbm.at[pl.ds(0, early_ref.shape[0])], early_ref, sems.at[2])
    lengths.start()
    table.start()
    early.start()
    lengths.wait()
    table.wait()
    slot = lax.axis_index("pool") * pages + lax.broadcasted_iota(jnp.int32, (pages, most_pages), 0)
    begin = page_len * lax.broadcasted_iota(jnp.int32, (1, most_pages), 1)
    code = jnp.zeros((pages, most_pages), jnp.int32)
    for r in range(requests):
        live = jnp.clip(length_ref[r] - begin, 0, page_len) + r * CODE
        code = jnp.where(table_ref[r : r + 1, :] == slot, live, code)
    code_ref[...] = jnp.sum(code.astype(jnp.float32).T, axis=0, keepdims=True).astype(jnp.int32)
    early.wait()


def attend_kernel(
    code_ref, q_ref, early_ref, k_hbm, v_hbm, out_ref, k_ref, v_ref, s_ref, mx_ref, sum_ref, acc_ref, sems
):
    pages, page_len, head_dim = v_ref.shape
    requests, group, _ = q_ref.shape
    early = early_ref.shape[0]
    factor = head_dim ** (-0.5) * LOG2E
    late = pltpu.make_async_copy(k_hbm.at[pl.ds(early, pages - early)], k_ref, sems.at[0])
    late.start()
    step = pages // CHUNKS
    blocks = [
        pltpu.make_async_copy(v_hbm.at[pl.ds(i * step, step)], v_ref.at[pl.ds(i * step, step)], sems.at[1 + i])
        for i in range(CHUNKS)
    ]
    for block in blocks:
        block.start()
    token = lax.broadcasted_iota(jnp.int32, (group, page_len), 1)
    halves = page_len // head_dim
    mx_ref[...] = jnp.full(mx_ref.shape, EMPTY, jnp.float32)
    sum_ref[...] = jnp.zeros(sum_ref.shape, jnp.float32)
    acc_ref[...] = jnp.zeros(acc_ref.shape, jnp.float32)

    def score(p, key_page):
        code = code_ref[0, p]
        owner = code // CODE
        s = lax.dot_general(
            q_ref[owner], key_page, (((1,), (1,)), ((), ())), preferred_element_type=jnp.float32
        )
        s = jnp.where(token < code % CODE, s, MASKED)
        s_ref[p] = s
        top = s[:, :head_dim]
        for h in range(1, halves):
            top = jnp.maximum(top, s[:, h * head_dim : (h + 1) * head_dim])
        mx_ref[owner] = jnp.maximum(mx_ref[owner], top)

    for p in range(early):
        score(p, early_ref[p])
    late.wait()
    for p in range(early, pages):
        score(p, k_ref[p - early])
    mx_ref[...] = jnp.broadcast_to(jnp.max(mx_ref[...], axis=-1, keepdims=True), mx_ref.shape)

    for i, block in enumerate(blocks):
        block.wait()
        for p in range(i * step, (i + 1) * step):
            owner = code_ref[0, p] // CODE
            top = mx_ref[owner]
            parts = [
                jnp.exp2((s_ref[p, :, h * head_dim : (h + 1) * head_dim] - top) * factor)
                for h in range(halves)
            ]
            sum_ref[owner] += sum(parts)
            weights = jnp.concatenate(parts, axis=1).astype(jnp.bfloat16)
            acc_ref[owner] += jnp.dot(weights, v_ref[p], preferred_element_type=jnp.float32)

    out_ref[:, :group, :] = acc_ref[...].astype(jnp.bfloat16)
    total = jnp.broadcast_to(jnp.sum(sum_ref[...], axis=-1, keepdims=True), sum_ref.shape)
    lane = lax.broadcasted_iota(jnp.int32, sum_ref.shape, 2)
    row = lax.broadcasted_iota(jnp.int32, sum_ref.shape, 1)
    stats = jnp.zeros(sum_ref.shape, jnp.float32)
    for k, part in enumerate(three_parts(mx_ref[...]) + three_parts(total)):
        stats = jnp.where(lane == row + k * group, part, stats)
    stats = jnp.sum(stats, axis=1, keepdims=True)
    out_ref[:, group:, :] = jnp.broadcast_to(stats, (requests, STAT_ROWS, head_dim)).astype(jnp.bfloat16)


def join_kernel(parts_ref, out_ref):
    sources, rows, head_dim = parts_ref.shape
    group = rows - STAT_ROWS
    factor = head_dim ** (-0.5) * LOG2E
    stats = parts_ref[:, group:, :].astype(jnp.float32)[:, 0, :]
    peak = stats[:, :group] + stats[:, group : 2 * group] + stats[:, 2 * group : 3 * group]
    total = (
        stats[:, 3 * group : 4 * group] + stats[:, 4 * group : 5 * group] + stats[:, 5 * group : 6 * group]
    )
    weight = jnp.exp2((peak - jnp.max(peak, axis=0, keepdims=True)) * factor)
    weight = weight / jnp.sum(weight * total, axis=0, keepdims=True)
    weight = weight.T
    result = jnp.zeros((group, head_dim), jnp.float32)
    for s in range(sources):
        result += weight[:, s : s + 1] * parts_ref[s, :group, :].astype(jnp.float32)
    for g in range(group):
        out_ref[0, :, g * head_dim : (g + 1) * head_dim] = result[g : g + 1, :].astype(jnp.bfloat16)


def per_device(queries, keys, values, page_table, lengths):
    pages, _, page_len, head_dim = keys.shape
    group = queries.shape[2] // head_dim
    requests = page_table.shape[0]
    vmem = pl.BlockSpec(memory_space=pltpu.VMEM)
    smem = pl.BlockSpec(memory_space=pltpu.SMEM)
    hbm = pl.BlockSpec(memory_space=pltpu.HBM)

    def stay(array):
        return pltpu.with_memory_space_constraint(array, pltpu.HBM)

    key_pages = keys.reshape(pages, page_len, head_dim)
    value_pages = values.reshape(pages, page_len, head_dim)
    spread = pl.pallas_call(
        spread_kernel,
        out_shape=jax.ShapeDtypeStruct((requests, group, head_dim), jnp.bfloat16),
        in_specs=[hbm],
        out_specs=vmem,
        scratch_shapes=[pltpu.VMEM(queries.shape, queries.dtype), pltpu.SemaphoreType.DMA],
        compiler_params=pltpu.CompilerParams(vmem_limit_bytes=4 * MIB),
    )(stay(queries))
    query_all = lax.all_to_all(spread, "pool", 0, 0, tiled=True)
    code, early = pl.pallas_call(
        prepare_kernel,
        out_shape=[
            jax.ShapeDtypeStruct((1, pages), jnp.int32),
            pltpu.VMEM((EARLY, page_len, head_dim), jnp.bfloat16),
        ],
        in_specs=[hbm, hbm, hbm],
        out_specs=[vmem, vmem],
        scratch_shapes=[
            pltpu.SMEM(lengths.shape, jnp.int32),
            pltpu.VMEM(page_table.shape, jnp.int32),
            pltpu.SemaphoreType.DMA((3,)),
        ],
        compiler_params=pltpu.CompilerParams(vmem_limit_bytes=8 * MIB),
        cost_estimate=pl.CostEstimate(
            flops=10**6, bytes_accessed=2 * EARLY * page_len * head_dim, transcendentals=0
        ),
    )(stay(lengths), stay(page_table), stay(key_pages))
    partial = pl.pallas_call(
        attend_kernel,
        out_shape=jax.ShapeDtypeStruct((requests, group + STAT_ROWS, head_dim), jnp.bfloat16),
        in_specs=[smem, vmem, vmem, hbm, hbm],
        out_specs=vmem,
        scratch_shapes=[
            pltpu.VMEM((pages - EARLY, page_len, head_dim), jnp.bfloat16),
            pltpu.VMEM((pages, page_len, head_dim), jnp.bfloat16),
            pltpu.VMEM((pages, group, page_len), jnp.float32),
            pltpu.VMEM((requests, group, head_dim), jnp.float32),
            pltpu.VMEM((requests, group, head_dim), jnp.float32),
            pltpu.VMEM((requests, group, head_dim), jnp.float32),
            pltpu.SemaphoreType.DMA((1 + CHUNKS,)),
        ],
        compiler_params=pltpu.CompilerParams(vmem_limit_bytes=24 * MIB),
    )(code, query_all, early, stay(key_pages), stay(value_pages))
    received = lax.all_to_all(partial, "pool", 0, 0, tiled=True)
    return pl.pallas_call(
        join_kernel,
        out_shape=jax.ShapeDtypeStruct((1, 1, group * head_dim), jnp.bfloat16),
        in_specs=[vmem],
        out_specs=vmem,
        compiler_params=pltpu.CompilerParams(vmem_limit_bytes=4 * MIB),
    )(received)


def solution(mesh):
    placed = (
        P("pool", "head", None),
        P("pool", "head", None, None),
        P("pool", "head", None, None),
        P(),
        P(),
    )
    return jax.shard_map(
        per_device, mesh=mesh, in_specs=placed, out_specs=P("pool", "head", None), check_vma=False
    )
```

```python
import jax
import jax.numpy as jnp
from jax import lax
from jax.experimental import pallas as pl
from jax.experimental.pallas import tpu as pltpu
from jax.sharding import PartitionSpec as P

MASKED = -3.0e38
EMPTY = -1.5e38
STAT_ROWS = 8
CODE = 512
EARLY = 48
CHUNKS = 2
MIB = 1024 * 1024
LOG2E = 1.4426950408889634


def three_parts(x):
    high = x.astype(jnp.bfloat16).astype(jnp.float32)
    rest = x - high
    middle = rest.astype(jnp.bfloat16).astype(jnp.float32)
    return high, middle, rest - middle


def spread_kernel(q_hbm, out_ref, q_ref, sem):
    _, group, head_dim = out_ref.shape
    copy = pltpu.make_async_copy(q_hbm, q_ref, sem)
    copy.start()
    copy.wait()
    rows = [q_ref[0, :, g * head_dim : (g + 1) * head_dim].astype(jnp.float32) for g in range(group)]
    tile = jnp.concatenate(rows, axis=0).astype(jnp.bfloat16)
    out_ref[...] = jnp.broadcast_to(tile[None], out_ref.shape)


def prepare_kernel(length_hbm, table_hbm, k_hbm, code_ref, early_ref, length_ref, table_ref, sems):
    pages, page_len, _ = k_hbm.shape
    requests, most_pages = table_ref.shape
    lengths = pltpu.make_async_copy(length_hbm, length_ref, sems.at[0])
    table = pltpu.make_async_copy(table_hbm, table_ref, sems.at[1])
    early = pltpu.make_async_copy(k_hbm.at[pl.ds(0, early_ref.shape[0])], early_ref, sems.at[2])
    lengths.start()
    table.start()
    early.start()
    lengths.wait()
    table.wait()
    slot = lax.axis_index("pool") * pages + lax.broadcasted_iota(jnp.int32, (pages, most_pages), 0)
    begin = page_len * lax.broadcasted_iota(jnp.int32, (1, most_pages), 1)
    code = jnp.zeros((pages, most_pages), jnp.int32)
    for r in range(requests):
        live = jnp.clip(length_ref[r] - begin, 0, page_len) + r * CODE
        code = jnp.where(table_ref[r : r + 1, :] == slot, live, code)
    code_ref[...] = jnp.sum(code.astype(jnp.float32).T, axis=0, keepdims=True).astype(jnp.int32)
    early.wait()


def attend_kernel(
    code_vmem, q_ref, early_ref, k_hbm, v_hbm, out_ref, code_ref, k_ref, v_ref, s_ref, mx_ref, sum_ref, acc_ref, sems
):
    pages, page_len, head_dim = v_ref.shape
    requests, group, _ = q_ref.shape
    early = early_ref.shape[0]
    factor = head_dim ** (-0.5) * LOG2E
    codes = pltpu.make_async_copy(code_vmem, code_ref, sems.at[1 + CHUNKS])
    codes.start()
    late = pltpu.make_async_copy(k_hbm.at[pl.ds(early, pages - early)], k_ref, sems.at[0])
    late.start()
    step = pages // CHUNKS
    blocks = [
        pltpu.make_async_copy(v_hbm.at[pl.ds(i * step, step)], v_ref.at[pl.ds(i * step, step)], sems.at[1 + i])
        for i in range(CHUNKS)
    ]
    for block in blocks:
        block.start()
    token = lax.broadcasted_iota(jnp.int32, (group, page_len), 1)
    halves = page_len // head_dim
    mx_ref[...] = jnp.full(mx_ref.shape, EMPTY, jnp.float32)
    sum_ref[...] = jnp.zeros(sum_ref.shape, jnp.float32)
    acc_ref[...] = jnp.zeros(acc_ref.shape, jnp.float32)

    codes.wait()

    def score(p, key_page):
        code = code_ref[0, p]
        owner = code // CODE
        s = lax.dot_general(
            q_ref[owner], key_page, (((1,), (1,)), ((), ())), preferred_element_type=jnp.float32
        )
        s = jnp.where(token < code % CODE, s, MASKED)
        s_ref[p] = s
        top = s[:, :head_dim]
        for h in range(1, halves):
            top = jnp.maximum(top, s[:, h * head_dim : (h + 1) * head_dim])
        mx_ref[owner] = jnp.maximum(mx_ref[owner], top)

    for p in range(early):
        score(p, early_ref[p])
    late.wait()
    for p in range(early, pages):
        score(p, k_ref[p - early])
    mx_ref[...] = jnp.broadcast_to(jnp.max(mx_ref[...], axis=-1, keepdims=True), mx_ref.shape)

    for i, block in enumerate(blocks):
        block.wait()
        for p in range(i * step, (i + 1) * step):
            owner = code_ref[0, p] // CODE
            top = mx_ref[owner]
            parts = [
                jnp.exp2((s_ref[p, :, h * head_dim : (h + 1) * head_dim] - top) * factor)
                for h in range(halves)
            ]
            sum_ref[owner] += sum(parts)
            weights = jnp.concatenate(parts, axis=1).astype(jnp.bfloat16)
            acc_ref[owner] += jnp.dot(weights, v_ref[p], preferred_element_type=jnp.float32)

    out_ref[:, :group, :] = acc_ref[...].astype(jnp.bfloat16)
    total = jnp.broadcast_to(jnp.sum(sum_ref[...], axis=-1, keepdims=True), sum_ref.shape)
    lane = lax.broadcasted_iota(jnp.int32, sum_ref.shape, 2)
    row = lax.broadcasted_iota(jnp.int32, sum_ref.shape, 1)
    stats = jnp.zeros(sum_ref.shape, jnp.float32)
    for k, part in enumerate(three_parts(mx_ref[...]) + three_parts(total)):
        stats = jnp.where(lane == row + k * group, part, stats)
    stats = jnp.sum(stats, axis=1, keepdims=True)
    out_ref[:, group:, :] = jnp.broadcast_to(stats, (requests, STAT_ROWS, head_dim)).astype(jnp.bfloat16)


def join_kernel(parts_ref, out_ref):
    sources, rows, head_dim = parts_ref.shape
    group = rows - STAT_ROWS
    factor = head_dim ** (-0.5) * LOG2E
    stats = parts_ref[:, group:, :].astype(jnp.float32)[:, 0, :]
    peak = stats[:, :group] + stats[:, group : 2 * group] + stats[:, 2 * group : 3 * group]
    total = (
        stats[:, 3 * group : 4 * group] + stats[:, 4 * group : 5 * group] + stats[:, 5 * group : 6 * group]
    )
    weight = jnp.exp2((peak - jnp.max(peak, axis=0, keepdims=True)) * factor)
    weight = weight / jnp.sum(weight * total, axis=0, keepdims=True)
    weight = weight.T
    result = jnp.zeros((group, head_dim), jnp.float32)
    for s in range(sources):
        result += weight[:, s : s + 1] * parts_ref[s, :group, :].astype(jnp.float32)
    for g in range(group):
        out_ref[0, :, g * head_dim : (g + 1) * head_dim] = result[g : g + 1, :].astype(jnp.bfloat16)


def per_device(queries, keys, values, page_table, lengths):
    pages, _, page_len, head_dim = keys.shape
    group = queries.shape[2] // head_dim
    requests = page_table.shape[0]
    vmem = pl.BlockSpec(memory_space=pltpu.VMEM)
    hbm = pl.BlockSpec(memory_space=pltpu.HBM)

    def stay(array):
        return pltpu.with_memory_space_constraint(array, pltpu.HBM)

    key_pages = keys.reshape(pages, page_len, head_dim)
    value_pages = values.reshape(pages, page_len, head_dim)
    spread = pl.pallas_call(
        spread_kernel,
        out_shape=jax.ShapeDtypeStruct((requests, group, head_dim), jnp.bfloat16),
        in_specs=[hbm],
        out_specs=vmem,
        scratch_shapes=[pltpu.VMEM(queries.shape, queries.dtype), pltpu.SemaphoreType.DMA],
        compiler_params=pltpu.CompilerParams(vmem_limit_bytes=4 * MIB),
    )(stay(queries))
    query_all = lax.all_to_all(spread, "pool", 0, 0, tiled=True)
    code, early = pl.pallas_call(
        prepare_kernel,
        out_shape=[
            jax.ShapeDtypeStruct((1, pages), jnp.int32),
            pltpu.VMEM((EARLY, page_len, head_dim), jnp.bfloat16),
        ],
        in_specs=[hbm, hbm, hbm],
        out_specs=[vmem, vmem],
        scratch_shapes=[
            pltpu.SMEM(lengths.shape, jnp.int32),
            pltpu.VMEM(page_table.shape, jnp.int32),
            pltpu.SemaphoreType.DMA((3,)),
        ],
        compiler_params=pltpu.CompilerParams(vmem_limit_bytes=8 * MIB),
        cost_estimate=pl.CostEstimate(
            flops=10**6, bytes_accessed=2 * EARLY * page_len * head_dim, transcendentals=0
        ),
    )(stay(lengths), stay(page_table), stay(key_pages))
    partial = pl.pallas_call(
        attend_kernel,
        out_shape=jax.ShapeDtypeStruct((requests, group + STAT_ROWS, head_dim), jnp.bfloat16),
        in_specs=[vmem, vmem, vmem, hbm, hbm],
        out_specs=vmem,
        scratch_shapes=[
            pltpu.SMEM((1, pages), jnp.int32),
            pltpu.VMEM((pages - EARLY, page_len, head_dim), jnp.bfloat16),
            pltpu.VMEM((pages, page_len, head_dim), jnp.bfloat16),
            pltpu.VMEM((pages, group, page_len), jnp.float32),
            pltpu.VMEM((requests, group, head_dim), jnp.float32),
            pltpu.VMEM((requests, group, head_dim), jnp.float32),
            pltpu.VMEM((requests, group, head_dim), jnp.float32),
            pltpu.SemaphoreType.DMA((2 + CHUNKS,)),
        ],
        compiler_params=pltpu.CompilerParams(vmem_limit_bytes=24 * MIB),
    )(code, query_all, early, stay(key_pages), stay(value_pages))
    received = lax.all_to_all(partial, "pool", 0, 0, tiled=True)
    return pl.pallas_call(
        join_kernel,
        out_shape=jax.ShapeDtypeStruct((1, 1, group * head_dim), jnp.bfloat16),
        in_specs=[vmem],
        out_specs=vmem,
        compiler_params=pltpu.CompilerParams(vmem_limit_bytes=4 * MIB),
    )(received)


def solution(mesh):
    placed = (
        P("pool", "head", None),
        P("pool", "head", None, None),
        P("pool", "head", None, None),
        P(),
        P(),
    )
    return jax.shard_map(
        per_device, mesh=mesh, in_specs=placed, out_specs=P("pool", "head", None), check_vma=False
    )
```

```python
import jax
import jax.numpy as jnp
from jax import lax
from jax.experimental import pallas as pl
from jax.experimental.pallas import tpu as pltpu
from jax.sharding import PartitionSpec as P

MASKED = -3.0e38
EMPTY = -1.5e38
STAT_ROWS = 8
CODE = 512
EARLY = 50
BLOCKS = (0, 32, 52, 64)
MIB = 1024 * 1024
LOG2E = 1.4426950408889634


def three_parts(x):
    high = x.astype(jnp.bfloat16).astype(jnp.float32)
    rest = x - high
    middle = rest.astype(jnp.bfloat16).astype(jnp.float32)
    return high, middle, rest - middle


def spread_kernel(q_hbm, out_ref, q_ref, sem):
    _, group, head_dim = out_ref.shape
    copy = pltpu.make_async_copy(q_hbm, q_ref, sem)
    copy.start()
    copy.wait()
    rows = [q_ref[0, :, g * head_dim : (g + 1) * head_dim].astype(jnp.float32) for g in range(group)]
    tile = jnp.concatenate(rows, axis=0).astype(jnp.bfloat16)
    out_ref[...] = jnp.broadcast_to(tile[None], out_ref.shape)


def prepare_kernel(length_hbm, table_hbm, k_hbm, code_ref, early_ref, length_ref, table_ref, row_ref, sems):
    pages, page_len, _ = k_hbm.shape
    requests, most_pages = table_ref.shape
    lengths = pltpu.make_async_copy(length_hbm, length_ref, sems.at[0])
    table = pltpu.make_async_copy(table_hbm, table_ref, sems.at[1])
    early = pltpu.make_async_copy(k_hbm.at[pl.ds(0, early_ref.shape[0])], early_ref, sems.at[2])
    lengths.start()
    table.start()
    early.start()
    lengths.wait()
    table.wait()
    slot = lax.axis_index("pool") * pages + lax.broadcasted_iota(jnp.int32, (pages, most_pages), 0)
    begin = page_len * lax.broadcasted_iota(jnp.int32, (1, most_pages), 1)
    code = jnp.zeros((pages, most_pages), jnp.int32)
    for r in range(requests):
        live = jnp.clip(length_ref[r] - begin, 0, page_len) + r * CODE
        code = jnp.where(table_ref[r : r + 1, :] == slot, live, code)
    row_ref[...] = jnp.sum(code.astype(jnp.float32).T, axis=0, keepdims=True).astype(jnp.int32)
    codes = pltpu.make_async_copy(row_ref, code_ref, sems.at[3])
    codes.start()
    codes.wait()
    early.wait()


def attend_kernel(
    code_ref, q_ref, early_ref, k_hbm, v_hbm, out_ref, k_ref, v_ref, s_ref, mx_ref, sum_ref, acc_ref, sems
):
    pages, page_len, head_dim = v_ref.shape
    requests, group, _ = q_ref.shape
    early = early_ref.shape[0]
    factor = head_dim ** (-0.5) * LOG2E
    late = pltpu.make_async_copy(k_hbm.at[pl.ds(early, pages - early)], k_ref, sems.at[0])
    late.start()
    bounds = list(zip(BLOCKS, BLOCKS[1:]))
    blocks = [
        pltpu.make_async_copy(v_hbm.at[pl.ds(lo, hi - lo)], v_ref.at[pl.ds(lo, hi - lo)], sems.at[2 + i])
        for i, (lo, hi) in enumerate(bounds)
    ]
    for block in blocks:
        block.start()
    token = lax.broadcasted_iota(jnp.int32, (group, page_len), 1)
    halves = page_len // head_dim

    @pl.when(code_ref[0, 0] >= 0)
    def _():
        mx_ref[...] = jnp.full(mx_ref.shape, EMPTY, jnp.float32)
        sum_ref[...] = jnp.zeros(sum_ref.shape, jnp.float32)
        acc_ref[...] = jnp.zeros(acc_ref.shape, jnp.float32)

    def score(p, key_page):
        code = code_ref[0, p]
        owner = code // CODE
        s = lax.dot_general(
            q_ref[owner], key_page, (((1,), (1,)), ((), ())), preferred_element_type=jnp.float32
        )
        s = jnp.where(token < code % CODE, s, MASKED)
        s_ref[p] = s
        top = s[:, :head_dim]
        for h in range(1, halves):
            top = jnp.maximum(top, s[:, h * head_dim : (h + 1) * head_dim])
        mx_ref[owner] = jnp.maximum(mx_ref[owner], top)

    for p in range(early):
        score(p, early_ref[p])
    late.wait()
    for p in range(early, pages):
        score(p, k_ref[p - early])
    mx_ref[...] = jnp.broadcast_to(jnp.max(mx_ref[...], axis=-1, keepdims=True), mx_ref.shape)

    for block, (lo, hi) in zip(blocks, bounds):
        block.wait()
        for p in range(lo, hi):
            owner = code_ref[0, p] // CODE
            top = mx_ref[owner]
            parts = [
                jnp.exp2((s_ref[p, :, h * head_dim : (h + 1) * head_dim] - top) * factor)
                for h in range(halves)
            ]
            sum_ref[owner] += sum(parts)
            weights = jnp.concatenate(parts, axis=1).astype(jnp.bfloat16)
            acc_ref[owner] += jnp.dot(weights, v_ref[p], preferred_element_type=jnp.float32)

    out_ref[:, :group, :] = acc_ref[...].astype(jnp.bfloat16)
    total = jnp.broadcast_to(jnp.sum(sum_ref[...], axis=-1, keepdims=True), sum_ref.shape)
    lane = lax.broadcasted_iota(jnp.int32, sum_ref.shape, 2)
    row = lax.broadcasted_iota(jnp.int32, sum_ref.shape, 1)
    stats = jnp.zeros(sum_ref.shape, jnp.float32)
    for k, part in enumerate(three_parts(mx_ref[...]) + three_parts(total)):
        stats = jnp.where(lane == row + k * group, part, stats)
    stats = jnp.sum(stats, axis=1, keepdims=True)
    out_ref[:, group:, :] = jnp.broadcast_to(stats, (requests, STAT_ROWS, head_dim)).astype(jnp.bfloat16)


def join_kernel(parts_ref, out_ref):
    sources, rows, head_dim = parts_ref.shape
    group = rows - STAT_ROWS
    factor = head_dim ** (-0.5) * LOG2E
    tiles = parts_ref[:, group:, :].astype(jnp.float32)
    place = lax.broadcasted_iota(jnp.int32, (STAT_ROWS, head_dim), 0)
    blocks = []
    for first in range(0, sources, STAT_ROWS):
        block = tiles[first]
        for k in range(1, STAT_ROWS):
            block = jnp.where(place == k, tiles[first + k], block)
        blocks.append(block)
    stats = jnp.concatenate(blocks, axis=0).T
    part = [stats[k * group : (k + 1) * group, :] for k in range(6)]
    peak = part[0] + part[1] + part[2]
    total = part[3] + part[4] + part[5]
    weight = jnp.exp2((peak - jnp.max(peak, axis=1, keepdims=True)) * factor)
    whole = jnp.sum(weight * total, axis=1, keepdims=True)
    sums = [jnp.zeros((group, head_dim), jnp.float32) for _ in range(4)]
    for s in range(sources):
        sums[s % 4] += weight[:, s : s + 1] * parts_ref[s, :group, :].astype(jnp.float32)
    result = ((sums[0] + sums[1]) + (sums[2] + sums[3])) / whole
    for g in range(group):
        out_ref[0, :, g * head_dim : (g + 1) * head_dim] = result[g : g + 1, :].astype(jnp.bfloat16)


def per_device(queries, keys, values, page_table, lengths):
    pages, _, page_len, head_dim = keys.shape
    group = queries.shape[2] // head_dim
    requests = page_table.shape[0]
    vmem = pl.BlockSpec(memory_space=pltpu.VMEM)
    hbm = pl.BlockSpec(memory_space=pltpu.HBM)
    smem = pl.BlockSpec(memory_space=pltpu.SMEM)

    def stay(array):
        return pltpu.with_memory_space_constraint(array, pltpu.HBM)

    key_pages = keys.reshape(pages, page_len, head_dim)
    value_pages = values.reshape(pages, page_len, head_dim)
    spread = pl.pallas_call(
        spread_kernel,
        out_shape=jax.ShapeDtypeStruct((requests, group, head_dim), jnp.bfloat16),
        in_specs=[hbm],
        out_specs=vmem,
        scratch_shapes=[pltpu.VMEM(queries.shape, queries.dtype), pltpu.SemaphoreType.DMA],
        compiler_params=pltpu.CompilerParams(vmem_limit_bytes=4 * MIB),
    )(stay(queries))
    query_all = lax.all_to_all(spread, "pool", 0, 0, tiled=True)
    code, early = pl.pallas_call(
        prepare_kernel,
        out_shape=[
            pltpu.SMEM((1, pages), jnp.int32),
            pltpu.VMEM((EARLY, page_len, head_dim), jnp.bfloat16),
        ],
        in_specs=[hbm, hbm, hbm],
        out_specs=[smem, vmem],
        scratch_shapes=[
            pltpu.SMEM(lengths.shape, jnp.int32),
            pltpu.VMEM(page_table.shape, jnp.int32),
            pltpu.VMEM((1, pages), jnp.int32),
            pltpu.SemaphoreType.DMA((4,)),
        ],
        compiler_params=pltpu.CompilerParams(vmem_limit_bytes=8 * MIB),
        cost_estimate=pl.CostEstimate(
            flops=10**6, bytes_accessed=2 * EARLY * page_len * head_dim, transcendentals=0
        ),
    )(stay(lengths), stay(page_table), stay(key_pages))
    partial = pl.pallas_call(
        attend_kernel,
        out_shape=jax.ShapeDtypeStruct((requests, group + STAT_ROWS, head_dim), jnp.bfloat16),
        in_specs=[smem, vmem, vmem, hbm, hbm],
        out_specs=vmem,
        scratch_shapes=[
            pltpu.VMEM((pages - EARLY, page_len, head_dim), jnp.bfloat16),
            pltpu.VMEM((pages, page_len, head_dim), jnp.bfloat16),
            pltpu.VMEM((pages, group, page_len), jnp.float32),
            pltpu.VMEM((requests, group, head_dim), jnp.float32),
            pltpu.VMEM((requests, group, head_dim), jnp.float32),
            pltpu.VMEM((requests, group, head_dim), jnp.float32),
            pltpu.SemaphoreType.DMA((1 + len(BLOCKS),)),
        ],
        compiler_params=pltpu.CompilerParams(vmem_limit_bytes=24 * MIB),
    )(pltpu.with_memory_space_constraint(code, pltpu.SMEM), query_all, early, stay(key_pages), stay(value_pages))
    received = lax.all_to_all(partial, "pool", 0, 0, tiled=True)
    return pl.pallas_call(
        join_kernel,
        out_shape=jax.ShapeDtypeStruct((1, 1, group * head_dim), jnp.bfloat16),
        in_specs=[vmem],
        out_specs=vmem,
        compiler_params=pltpu.CompilerParams(vmem_limit_bytes=4 * MIB),
    )(received)


def solution(mesh):
    placed = (
        P("pool", "head", None),
        P("pool", "head", None, None),
        P("pool", "head", None, None),
        P(),
        P(),
    )
    return jax.shard_map(
        per_device, mesh=mesh, in_specs=placed, out_specs=P("pool", "head", None), check_vma=False
    )
```

```python
import jax
import jax.numpy as jnp
from jax import lax
from jax.experimental import pallas as pl
from jax.experimental.pallas import tpu as pltpu
from jax.sharding import PartitionSpec as P

MASKED = -3.0e38
EMPTY = -1.5e38
STAT_ROWS = 8
CODE = 512
PAGE = 256
MIB = 1024 * 1024
LOG2E = 1.4426950408889634


def three_parts(x):
    high = x.astype(jnp.bfloat16).astype(jnp.float32)
    rest = x - high
    middle = rest.astype(jnp.bfloat16).astype(jnp.float32)
    return high, middle, rest - middle


def spread_kernel(q_hbm, length_hbm, table_hbm, out_ref, code_ref, q_ref, length_ref, table_ref, row_ref, sems):
    requests, group, head_dim = out_ref.shape
    pages = code_ref.shape[1]
    most_pages = table_ref.shape[1]
    lengths = pltpu.make_async_copy(length_hbm, length_ref, sems.at[0])
    table = pltpu.make_async_copy(table_hbm, table_ref, sems.at[1])
    query = pltpu.make_async_copy(q_hbm, q_ref, sems.at[2])
    lengths.start()
    table.start()
    query.start()
    lengths.wait()
    table.wait()
    slot = lax.axis_index("pool") * pages + lax.broadcasted_iota(jnp.int32, (pages, most_pages), 0)
    begin = PAGE * lax.broadcasted_iota(jnp.int32, (1, most_pages), 1)
    code = jnp.zeros((pages, most_pages), jnp.int32)
    for r in range(requests):
        live = jnp.clip(length_ref[r] - begin, 0, PAGE) + r * CODE
        code = jnp.where(table_ref[r : r + 1, :] == slot, live, code)
    row_ref[...] = jnp.sum(code.astype(jnp.float32).T, axis=0, keepdims=True).astype(jnp.int32)
    codes = pltpu.make_async_copy(row_ref, code_ref, sems.at[3])
    codes.start()
    query.wait()
    rows = [q_ref[0, :, g * head_dim : (g + 1) * head_dim].astype(jnp.float32) for g in range(group)]
    tile = jnp.concatenate(rows, axis=0).astype(jnp.bfloat16)
    out_ref[...] = jnp.broadcast_to(tile[None], out_ref.shape)
    codes.wait()


def attend_kernel(code_ref, q_ref, k_ref, v_ref, out_ref, s_ref, mx_ref, sum_ref, acc_ref):
    pages, page_len, head_dim = k_ref.shape
    requests, group, _ = q_ref.shape
    factor = head_dim ** (-0.5) * LOG2E
    token = lax.broadcasted_iota(jnp.int32, (group, page_len), 1)
    halves = page_len // head_dim

    mx_ref[...] = jnp.full(mx_ref.shape, EMPTY, jnp.float32)
    sum_ref[...] = jnp.zeros(sum_ref.shape, jnp.float32)
    acc_ref[...] = jnp.zeros(acc_ref.shape, jnp.float32)

    def score(p, key_page):
        code = code_ref[0, p]
        owner = code // CODE
        s = lax.dot_general(
            q_ref[owner], key_page, (((1,), (1,)), ((), ())), preferred_element_type=jnp.float32
        )
        s = jnp.where(token < code % CODE, s, MASKED)
        s_ref[p] = s
        top = s[:, :head_dim]
        for h in range(1, halves):
            top = jnp.maximum(top, s[:, h * head_dim : (h + 1) * head_dim])
        mx_ref[owner] = jnp.maximum(mx_ref[owner], top)

    for p in range(pages):
        score(p, k_ref[p])
    mx_ref[...] = jnp.broadcast_to(jnp.max(mx_ref[...], axis=-1, keepdims=True), mx_ref.shape)

    for p in range(pages):
        owner = code_ref[0, p] // CODE
        top = mx_ref[owner]
        parts = [
            jnp.exp2((s_ref[p, :, h * head_dim : (h + 1) * head_dim] - top) * factor)
            for h in range(halves)
        ]
        sum_ref[owner] += sum(parts)
        weights = jnp.concatenate(parts, axis=1).astype(jnp.bfloat16)
        acc_ref[owner] += jnp.dot(weights, v_ref[p], preferred_element_type=jnp.float32)

    out_ref[:, :group, :] = acc_ref[...].astype(jnp.bfloat16)
    total = jnp.broadcast_to(jnp.sum(sum_ref[...], axis=-1, keepdims=True), sum_ref.shape)
    lane = lax.broadcasted_iota(jnp.int32, sum_ref.shape, 2)
    row = lax.broadcasted_iota(jnp.int32, sum_ref.shape, 1)
    stats = jnp.zeros(sum_ref.shape, jnp.float32)
    for k, part in enumerate(three_parts(mx_ref[...]) + three_parts(total)):
        stats = jnp.where(lane == row + k * group, part, stats)
    stats = jnp.sum(stats, axis=1, keepdims=True)
    out_ref[:, group:, :] = jnp.broadcast_to(stats, (requests, STAT_ROWS, head_dim)).astype(jnp.bfloat16)


def join_kernel(parts_ref, out_ref):
    sources, rows, head_dim = parts_ref.shape
    group = rows - STAT_ROWS
    factor = head_dim ** (-0.5) * LOG2E
    tiles = parts_ref[:, group:, :].astype(jnp.float32)
    place = lax.broadcasted_iota(jnp.int32, (STAT_ROWS, head_dim), 0)
    blocks = []
    for first in range(0, sources, STAT_ROWS):
        block = tiles[first]
        for k in range(1, STAT_ROWS):
            block = jnp.where(place == k, tiles[first + k], block)
        blocks.append(block)
    stats = jnp.concatenate(blocks, axis=0).T
    part = [stats[k * group : (k + 1) * group, :] for k in range(6)]
    peak = part[0] + part[1] + part[2]
    total = part[3] + part[4] + part[5]
    weight = jnp.exp2((peak - jnp.max(peak, axis=1, keepdims=True)) * factor)
    whole = jnp.sum(weight * total, axis=1, keepdims=True)
    sums = [jnp.zeros((group, head_dim), jnp.float32) for _ in range(4)]
    for s in range(sources):
        sums[s % 4] += weight[:, s : s + 1] * parts_ref[s, :group, :].astype(jnp.float32)
    result = ((sums[0] + sums[1]) + (sums[2] + sums[3])) / whole
    for g in range(group):
        out_ref[0, :, g * head_dim : (g + 1) * head_dim] = result[g : g + 1, :].astype(jnp.bfloat16)


def per_device(queries, keys, values, page_table, lengths):
    pages, _, page_len, head_dim = keys.shape
    group = queries.shape[2] // head_dim
    requests = page_table.shape[0]
    vmem = pl.BlockSpec(memory_space=pltpu.VMEM)
    hbm = pl.BlockSpec(memory_space=pltpu.HBM)
    smem = pl.BlockSpec(memory_space=pltpu.SMEM)

    def stay(array):
        return pltpu.with_memory_space_constraint(array, pltpu.HBM)

    key_pages = keys.reshape(pages, page_len, head_dim)
    value_pages = values.reshape(pages, page_len, head_dim)
    spread, code = pl.pallas_call(
        spread_kernel,
        out_shape=[
            jax.ShapeDtypeStruct((requests, group, head_dim), jnp.bfloat16),
            pltpu.SMEM((1, pages), jnp.int32),
        ],
        in_specs=[hbm, hbm, hbm],
        out_specs=[vmem, smem],
        scratch_shapes=[
            pltpu.VMEM(queries.shape, queries.dtype),
            pltpu.SMEM(lengths.shape, jnp.int32),
            pltpu.VMEM(page_table.shape, jnp.int32),
            pltpu.VMEM((1, pages), jnp.int32),
            pltpu.SemaphoreType.DMA((4,)),
        ],
        compiler_params=pltpu.CompilerParams(vmem_limit_bytes=4 * MIB),
        cost_estimate=pl.CostEstimate(flops=2 * 10**10, bytes_accessed=64 * MIB, transcendentals=0),
    )(stay(queries), stay(lengths), stay(page_table))
    query_all = lax.all_to_all(spread, "pool", 0, 0, tiled=True)
    partial = pl.pallas_call(
        attend_kernel,
        out_shape=jax.ShapeDtypeStruct((requests, group + STAT_ROWS, head_dim), jnp.bfloat16),
        in_specs=[smem, vmem, vmem, vmem],
        out_specs=vmem,
        scratch_shapes=[
            pltpu.VMEM((pages, group, page_len), jnp.float32),
            pltpu.VMEM((requests, group, head_dim), jnp.float32),
            pltpu.VMEM((requests, group, head_dim), jnp.float32),
            pltpu.VMEM((requests, group, head_dim), jnp.float32),
        ],
        compiler_params=pltpu.CompilerParams(vmem_limit_bytes=24 * MIB),
    )(pltpu.with_memory_space_constraint(code, pltpu.SMEM), query_all, key_pages, value_pages)
    received = lax.all_to_all(partial, "pool", 0, 0, tiled=True)
    return pl.pallas_call(
        join_kernel,
        out_shape=jax.ShapeDtypeStruct((1, 1, group * head_dim), jnp.bfloat16),
        in_specs=[vmem],
        out_specs=vmem,
        compiler_params=pltpu.CompilerParams(vmem_limit_bytes=4 * MIB),
    )(received)


def solution(mesh):
    placed = (
        P("pool", "head", None),
        P("pool", "head", None, None),
        P("pool", "head", None, None),
        P(),
        P(),
    )
    return jax.shard_map(
        per_device, mesh=mesh, in_specs=placed, out_specs=P("pool", "head", None), check_vma=False
    )
```

```python
import jax
import jax.numpy as jnp
from jax import lax
from jax.experimental import pallas as pl
from jax.experimental.pallas import tpu as pltpu
from jax.sharding import PartitionSpec as P

MASKED = -3.0e38
EMPTY = -1.5e38
STAT_ROWS = 8
CODE = 512
PAGE = 256
MIB = 1024 * 1024
LOG2E = 1.4426950408889634


def three_parts(x):
    high = x.astype(jnp.bfloat16).astype(jnp.float32)
    rest = x - high
    middle = rest.astype(jnp.bfloat16).astype(jnp.float32)
    return high, middle, rest - middle


def spread_kernel(q_hbm, length_hbm, table_hbm, out_ref, code_ref, q_ref, length_ref, table_ref, sems):
    requests, group, head_dim = out_ref.shape
    pages = code_ref.shape[1]
    most_pages = table_ref.shape[1]
    lengths = pltpu.make_async_copy(length_hbm, length_ref, sems.at[0])
    table = pltpu.make_async_copy(table_hbm, table_ref, sems.at[1])
    query = pltpu.make_async_copy(q_hbm, q_ref, sems.at[2])
    lengths.start()
    table.start()
    query.start()
    lengths.wait()
    table.wait()
    slot = lax.axis_index("pool") * pages + lax.broadcasted_iota(jnp.int32, (pages, most_pages), 0)
    begin = PAGE * lax.broadcasted_iota(jnp.int32, (1, most_pages), 1)
    code = jnp.zeros((pages, most_pages), jnp.int32)
    for r in range(requests):
        live = jnp.clip(length_ref[r] - begin, 0, PAGE) + r * CODE
        code = jnp.where(table_ref[r : r + 1, :] == slot, live, code)
    code_ref[...] = jnp.sum(code.astype(jnp.float32).T, axis=0, keepdims=True).astype(jnp.int32)
    query.wait()
    rows = [q_ref[0, :, g * head_dim : (g + 1) * head_dim].astype(jnp.float32) for g in range(group)]
    tile = jnp.concatenate(rows, axis=0).astype(jnp.bfloat16)
    out_ref[...] = jnp.broadcast_to(tile[None], out_ref.shape)


def attend_kernel(code_ref, q_ref, k_ref, v_ref, out_ref, s_ref, mx_ref, sum_ref, acc_ref):
    pages, page_len, head_dim = k_ref.shape
    requests, group, _ = q_ref.shape
    factor = head_dim ** (-0.5) * LOG2E
    listed = code_ref[...]
    codes = [listed[0, p] for p in range(pages)]
    token = lax.broadcasted_iota(jnp.int32, (group, page_len), 1)
    halves = page_len // head_dim

    mx_ref[...] = jnp.full(mx_ref.shape, EMPTY, jnp.float32)
    sum_ref[...] = jnp.zeros(sum_ref.shape, jnp.float32)
    acc_ref[...] = jnp.zeros(acc_ref.shape, jnp.float32)

    def score(p, key_page):
        code = codes[p]
        owner = code // CODE
        s = lax.dot_general(
            q_ref[owner], key_page, (((1,), (1,)), ((), ())), preferred_element_type=jnp.float32
        )
        s = jnp.where(token < code % CODE, s, MASKED)
        s_ref[p] = s
        top = s[:, :head_dim]
        for h in range(1, halves):
            top = jnp.maximum(top, s[:, h * head_dim : (h + 1) * head_dim])
        mx_ref[owner] = jnp.maximum(mx_ref[owner], top)

    for p in range(pages):
        score(p, k_ref[p])
    mx_ref[...] = jnp.broadcast_to(jnp.max(mx_ref[...], axis=-1, keepdims=True), mx_ref.shape)

    for p in range(pages):
        owner = codes[p] // CODE
        top = mx_ref[owner]
        parts = [
            jnp.exp2((s_ref[p, :, h * head_dim : (h + 1) * head_dim] - top) * factor)
            for h in range(halves)
        ]
        sum_ref[owner] += sum(parts)
        weights = jnp.concatenate(parts, axis=1).astype(jnp.bfloat16)
        acc_ref[owner] += jnp.dot(weights, v_ref[p], preferred_element_type=jnp.float32)

    out_ref[:, :group, :] = acc_ref[...].astype(jnp.bfloat16)
    total = jnp.broadcast_to(jnp.sum(sum_ref[...], axis=-1, keepdims=True), sum_ref.shape)
    lane = lax.broadcasted_iota(jnp.int32, sum_ref.shape, 2)
    row = lax.broadcasted_iota(jnp.int32, sum_ref.shape, 1)
    stats = jnp.zeros(sum_ref.shape, jnp.float32)
    for k, part in enumerate(three_parts(mx_ref[...]) + three_parts(total)):
        stats = jnp.where(lane == row + k * group, part, stats)
    stats = jnp.sum(stats, axis=1, keepdims=True)
    out_ref[:, group:, :] = jnp.broadcast_to(stats, (requests, STAT_ROWS, head_dim)).astype(jnp.bfloat16)


def join_kernel(parts_ref, out_ref):
    sources, rows, head_dim = parts_ref.shape
    group = rows - STAT_ROWS
    factor = head_dim ** (-0.5) * LOG2E
    tiles = parts_ref[:, group:, :].astype(jnp.float32)
    place = lax.broadcasted_iota(jnp.int32, (STAT_ROWS, head_dim), 0)
    blocks = []
    for first in range(0, sources, STAT_ROWS):
        block = tiles[first]
        for k in range(1, STAT_ROWS):
            block = jnp.where(place == k, tiles[first + k], block)
        blocks.append(block)
    stats = jnp.concatenate(blocks, axis=0).T
    part = [stats[k * group : (k + 1) * group, :] for k in range(6)]
    peak = part[0] + part[1] + part[2]
    total = part[3] + part[4] + part[5]
    weight = jnp.exp2((peak - jnp.max(peak, axis=1, keepdims=True)) * factor)
    whole = jnp.sum(weight * total, axis=1, keepdims=True)
    sums = [jnp.zeros((group, head_dim), jnp.float32) for _ in range(4)]
    for s in range(sources):
        sums[s % 4] += weight[:, s : s + 1] * parts_ref[s, :group, :].astype(jnp.float32)
    result = ((sums[0] + sums[1]) + (sums[2] + sums[3])) / whole
    for g in range(group):
        out_ref[0, :, g * head_dim : (g + 1) * head_dim] = result[g : g + 1, :].astype(jnp.bfloat16)


def per_device(queries, keys, values, page_table, lengths):
    pages, _, page_len, head_dim = keys.shape
    group = queries.shape[2] // head_dim
    requests = page_table.shape[0]
    vmem = pl.BlockSpec(memory_space=pltpu.VMEM)
    hbm = pl.BlockSpec(memory_space=pltpu.HBM)

    def stay(array):
        return pltpu.with_memory_space_constraint(array, pltpu.HBM)

    key_pages = keys.reshape(pages, page_len, head_dim)
    value_pages = values.reshape(pages, page_len, head_dim)
    spread, code = pl.pallas_call(
        spread_kernel,
        out_shape=[
            jax.ShapeDtypeStruct((requests, group, head_dim), jnp.bfloat16),
            jax.ShapeDtypeStruct((1, pages), jnp.int32),
        ],
        in_specs=[hbm, hbm, hbm],
        out_specs=[vmem, vmem],
        scratch_shapes=[
            pltpu.VMEM(queries.shape, queries.dtype),
            pltpu.SMEM(lengths.shape, jnp.int32),
            pltpu.VMEM(page_table.shape, jnp.int32),
            pltpu.SemaphoreType.DMA((3,)),
        ],
        compiler_params=pltpu.CompilerParams(vmem_limit_bytes=4 * MIB),
        cost_estimate=pl.CostEstimate(flops=2 * 10**10, bytes_accessed=64 * MIB, transcendentals=0),
    )(stay(queries), stay(lengths), stay(page_table))
    query_all = lax.all_to_all(spread, "pool", 0, 0, tiled=True)
    partial = pl.pallas_call(
        attend_kernel,
        out_shape=jax.ShapeDtypeStruct((requests, group + STAT_ROWS, head_dim), jnp.bfloat16),
        in_specs=[vmem, vmem, vmem, vmem],
        out_specs=vmem,
        scratch_shapes=[
            pltpu.VMEM((pages, group, page_len), jnp.float32),
            pltpu.VMEM((requests, group, head_dim), jnp.float32),
            pltpu.VMEM((requests, group, head_dim), jnp.float32),
            pltpu.VMEM((requests, group, head_dim), jnp.float32),
        ],
        compiler_params=pltpu.CompilerParams(vmem_limit_bytes=24 * MIB),
    )(code, query_all, key_pages, value_pages)
    received = lax.all_to_all(partial, "pool", 0, 0, tiled=True)
    return pl.pallas_call(
        join_kernel,
        out_shape=jax.ShapeDtypeStruct((1, 1, group * head_dim), jnp.bfloat16),
        in_specs=[vmem],
        out_specs=vmem,
        compiler_params=pltpu.CompilerParams(vmem_limit_bytes=4 * MIB),
    )(received)


def solution(mesh):
    placed = (
        P("pool", "head", None),
        P("pool", "head", None, None),
        P("pool", "head", None, None),
        P(),
        P(),
    )
    return jax.shard_map(
        per_device, mesh=mesh, in_specs=placed, out_specs=P("pool", "head", None), check_vma=False
    )
```

```python
import jax
import jax.numpy as jnp
from jax import lax
from jax.experimental import pallas as pl
from jax.experimental.pallas import tpu as pltpu
from jax.sharding import PartitionSpec as P

MASKED = -3.0e38
EMPTY = -1.5e38
STAT_ROWS = 8
CODE_BITS = 9
CODE = 1 << CODE_BITS
PAGE = 256
MIB = 1024 * 1024
LOG2E = 1.4426950408889634


def three_parts(x):
    high = x.astype(jnp.bfloat16).astype(jnp.float32)
    rest = x - high
    middle = rest.astype(jnp.bfloat16).astype(jnp.float32)
    return high, middle, rest - middle


def spread_kernel(q_hbm, length_hbm, table_hbm, out_ref, code_ref, q_ref, length_ref, table_ref, sems):
    requests, group, head_dim = out_ref.shape
    pages = code_ref.shape[1]
    most_pages = table_ref.shape[1]
    lengths = pltpu.make_async_copy(length_hbm, length_ref, sems.at[0])
    table = pltpu.make_async_copy(table_hbm, table_ref, sems.at[1])
    query = pltpu.make_async_copy(q_hbm, q_ref, sems.at[2])
    lengths.start()
    table.start()
    query.start()
    lengths.wait()
    table.wait()
    slot = lax.axis_index("pool") * pages + lax.broadcasted_iota(jnp.int32, (pages, most_pages), 0)
    begin = PAGE * lax.broadcasted_iota(jnp.int32, (1, most_pages), 1)
    code = jnp.zeros((pages, most_pages), jnp.int32)
    for r in range(requests):
        live = jnp.clip(length_ref[r] - begin, 0, PAGE) + r * CODE
        code = jnp.where(table_ref[r : r + 1, :] == slot, live, code)
    code_ref[...] = jnp.sum(code.astype(jnp.float32).T, axis=0, keepdims=True).astype(jnp.int32)
    query.wait()
    rows = [q_ref[0, :, g * head_dim : (g + 1) * head_dim].astype(jnp.float32) for g in range(group)]
    tile = jnp.concatenate(rows, axis=0).astype(jnp.bfloat16)
    out_ref[...] = jnp.broadcast_to(tile[None], out_ref.shape)


def attend_kernel(code_ref, q_ref, k_ref, v_ref, out_ref, s_ref, mx_ref, sum_ref, acc_ref):
    pages, page_len, head_dim = k_ref.shape
    requests, group, _ = q_ref.shape
    factor = head_dim ** (-0.5) * LOG2E
    listed = code_ref[...]
    codes = [listed[0, p] for p in range(pages)]
    token = lax.broadcasted_iota(jnp.int32, (group, page_len), 1)
    halves = page_len // head_dim

    mx_ref[...] = jnp.full(mx_ref.shape, EMPTY, jnp.float32)
    sum_ref[...] = jnp.zeros(sum_ref.shape, jnp.float32)
    acc_ref[...] = jnp.zeros(acc_ref.shape, jnp.float32)

    def score(p, key_page):
        code = codes[p]
        owner = code >> CODE_BITS
        s = lax.dot_general(
            q_ref[owner], key_page, (((1,), (1,)), ((), ())), preferred_element_type=jnp.float32
        )
        s = jnp.where(token < code & (CODE - 1), s, MASKED)
        s_ref[p] = s
        top = s[:, :head_dim]
        for h in range(1, halves):
            top = jnp.maximum(top, s[:, h * head_dim : (h + 1) * head_dim])
        mx_ref[owner] = jnp.maximum(mx_ref[owner], top)

    for p in range(pages):
        score(p, k_ref[p])
    mx_ref[...] = jnp.broadcast_to(jnp.max(mx_ref[...], axis=-1, keepdims=True), mx_ref.shape)

    for p in range(pages):
        owner = codes[p] >> CODE_BITS
        top = mx_ref[owner]
        parts = [
            jnp.exp2((s_ref[p, :, h * head_dim : (h + 1) * head_dim] - top) * factor)
            for h in range(halves)
        ]
        sum_ref[owner] += sum(parts)
        weights = jnp.concatenate(parts, axis=1).astype(jnp.bfloat16)
        acc_ref[owner] += jnp.dot(weights, v_ref[p], preferred_element_type=jnp.float32)

    out_ref[:, :group, :] = acc_ref[...].astype(jnp.bfloat16)
    total = jnp.broadcast_to(jnp.sum(sum_ref[...], axis=-1, keepdims=True), sum_ref.shape)
    lane = lax.broadcasted_iota(jnp.int32, sum_ref.shape, 2)
    row = lax.broadcasted_iota(jnp.int32, sum_ref.shape, 1)
    stats = jnp.zeros(sum_ref.shape, jnp.float32)
    for k, part in enumerate(three_parts(mx_ref[...]) + three_parts(total)):
        stats = jnp.where(lane == row + k * group, part, stats)
    stats = jnp.sum(stats, axis=1, keepdims=True)
    out_ref[:, group:, :] = jnp.broadcast_to(stats, (requests, STAT_ROWS, head_dim)).astype(jnp.bfloat16)


def join_kernel(parts_ref, out_ref):
    sources, rows, head_dim = parts_ref.shape
    group = rows - STAT_ROWS
    factor = head_dim ** (-0.5) * LOG2E
    tiles = parts_ref[:, group:, :].astype(jnp.float32)
    place = lax.broadcasted_iota(jnp.int32, (STAT_ROWS, head_dim), 0)
    blocks = []
    for first in range(0, sources, STAT_ROWS):
        block = tiles[first]
        for k in range(1, STAT_ROWS):
            block = jnp.where(place == k, tiles[first + k], block)
        blocks.append(block)
    stats = jnp.concatenate(blocks, axis=0).T
    part = [stats[k * group : (k + 1) * group, :] for k in range(6)]
    peak = part[0] + part[1] + part[2]
    total = part[3] + part[4] + part[5]
    weight = jnp.exp2((peak - jnp.max(peak, axis=1, keepdims=True)) * factor)
    whole = jnp.sum(weight * total, axis=1, keepdims=True)
    sums = [jnp.zeros((group, head_dim), jnp.float32) for _ in range(4)]
    for s in range(sources):
        sums[s % 4] += weight[:, s : s + 1] * parts_ref[s, :group, :].astype(jnp.float32)
    result = ((sums[0] + sums[1]) + (sums[2] + sums[3])) / whole
    for g in range(group):
        out_ref[0, :, g * head_dim : (g + 1) * head_dim] = result[g : g + 1, :].astype(jnp.bfloat16)


def per_device(queries, keys, values, page_table, lengths):
    pages, _, page_len, head_dim = keys.shape
    group = queries.shape[2] // head_dim
    requests = page_table.shape[0]
    vmem = pl.BlockSpec(memory_space=pltpu.VMEM)
    hbm = pl.BlockSpec(memory_space=pltpu.HBM)

    def stay(array):
        return pltpu.with_memory_space_constraint(array, pltpu.HBM)

    key_pages = keys.reshape(pages, page_len, head_dim)
    value_pages = values.reshape(pages, page_len, head_dim)
    spread, code = pl.pallas_call(
        spread_kernel,
        out_shape=[
            jax.ShapeDtypeStruct((requests, group, head_dim), jnp.bfloat16),
            jax.ShapeDtypeStruct((1, pages), jnp.int32),
        ],
        in_specs=[hbm, hbm, hbm],
        out_specs=[vmem, vmem],
        scratch_shapes=[
            pltpu.VMEM(queries.shape, queries.dtype),
            pltpu.SMEM(lengths.shape, jnp.int32),
            pltpu.VMEM(page_table.shape, jnp.int32),
            pltpu.SemaphoreType.DMA((3,)),
        ],
        compiler_params=pltpu.CompilerParams(vmem_limit_bytes=4 * MIB),
        cost_estimate=pl.CostEstimate(flops=2 * 10**10, bytes_accessed=64 * MIB, transcendentals=0),
    )(stay(queries), stay(lengths), stay(page_table))
    query_all = lax.all_to_all(spread, "pool", 0, 0, tiled=True)
    partial = pl.pallas_call(
        attend_kernel,
        out_shape=jax.ShapeDtypeStruct((requests, group + STAT_ROWS, head_dim), jnp.bfloat16),
        in_specs=[vmem, vmem, vmem, vmem],
        out_specs=vmem,
        scratch_shapes=[
            pltpu.VMEM((pages, group, page_len), jnp.float32),
            pltpu.VMEM((requests, group, head_dim), jnp.float32),
            pltpu.VMEM((requests, group, head_dim), jnp.float32),
            pltpu.VMEM((requests, group, head_dim), jnp.float32),
        ],
        compiler_params=pltpu.CompilerParams(vmem_limit_bytes=24 * MIB),
    )(code, query_all, key_pages, value_pages)
    received = lax.all_to_all(partial, "pool", 0, 0, tiled=True)
    return pl.pallas_call(
        join_kernel,
        out_shape=jax.ShapeDtypeStruct((1, 1, group * head_dim), jnp.bfloat16),
        in_specs=[vmem],
        out_specs=vmem,
        compiler_params=pltpu.CompilerParams(vmem_limit_bytes=4 * MIB),
    )(received)


def solution(mesh):
    placed = (
        P("pool", "head", None),
        P("pool", "head", None, None),
        P("pool", "head", None, None),
        P(),
        P(),
    )
    return jax.shard_map(
        per_device, mesh=mesh, in_specs=placed, out_specs=P("pool", "head", None), check_vma=False
    )
```
